32 devices in a mesh: group: 2 (over y), sub: 4 (over z), tile: 2 (over x), rep: 2 (over core).
Axes of the slice: x: 2, y: 2, z: 4, core: 2. Of those that a mesh axis runs over, the one named last changes fastest.
Arguments:
- right_side: bfloat16 [16, 1024, 512], P(('group', 'sub', 'tile'), None, 'rep'), parts along dimension 0, may hold values from -6 to 6
- interface_inverse: bfloat16 [16, 1024, 1024], P(('group', 'sub', 'tile')), parts along dimension 0, may hold values from -0.1875 to 0.1875
- coupling: float32 [16, 2, 128], P(('group', 'sub', 'tile')), parts along dimension 0, may hold values from 0.5 to 2
- trace_rows: int32 [16, 2, 128], P(('group', 'sub', 'tile')), parts along dimension 0, may hold values from 0 to 1023
- deflation_basis: bfloat16 [16, 1024, 128], P(('group', 'sub', 'tile')), parts along dimension 0, may hold values from -0.375 to 0.375
- deflation_counts: int32 [16], P(('group', 'sub', 'tile')), parts along dimension 0, may hold values from 32 to 128, as said below
- coarse_inverse: bfloat16 [8, 2, 128, 4, 256], P('group', 'tile', 'rep', 'sub'), parts along dimension 0, may hold values from -0.25 to 0.25
Outputs:
- corrected_field: bfloat16 [16, 1024, 512], P(('group', 'sub', 'tile'), None, 'rep'), parts along dimension 0
The draws below stay inside these ranges and needn't reach their ends.
There are 2 independent parts, one for each index of `group`. The reference program is written for one: setup_inputs(seed, part) draws one part's arguments, and reference() takes and returns one part's arrays. A program takes and returns all parts, laid end to end along the dimension named above; each array names one. Nothing has to cross between parts.
Inputs may be any that keep to these rules, and one draw needn't show every extreme that they name: `deflation_counts`: some subdomain has exactly 128 live deflation vectors.
All inputs are finite; a program needn't handle non-finite values.
Results may differ from the reference program's by a relative error of at most 0.035.
Values may be sent and summed in bfloat16 or wider, within the bound.
A program may use at most 64 MiB of HBM per device.

```python
import jax
import jax.numpy as jnp
from jax import lax

IFACE_ROWS = 1024
FACE_ROWS = 128
DEFL_SLOTS = 128
ROUNDS = 2
SUBDOMAINS = 8
ALL_MODES = 512
COARSE_ORDER = 1024
N_SUB = 4
N_TILE = 2


def draw_deflation_counts(key, part):
    key_counts, key_fullest = jax.random.split(jax.random.fold_in(key, 11))
    counts = jax.random.randint(key_counts, (SUBDOMAINS,), DEFL_SLOTS // 4, DEFL_SLOTS + 1, dtype=jnp.int32)
    fullest = jax.random.randint(key_fullest, (), 0, SUBDOMAINS, dtype=jnp.int32)
    positions = jnp.arange(SUBDOMAINS, dtype=jnp.int32)
    return jnp.where(positions == fullest, DEFL_SLOTS, counts).astype(jnp.int32)


def touch_ends(values, rng, low, largest):
    dims = values.shape
    spot = [jax.random.randint(jax.random.fold_in(rng, axis), (), 0, dims[axis]) for axis in range(len(dims))]
    values = values.at[tuple(spot)].set(low)
    longest = dims.index(max(dims))
    spot[longest] = (spot[longest] + 1) % dims[longest]
    return values.at[tuple(spot)].set(largest)


def raised(entries, stream_key, source, target, parts, factor):
    def block_of(position):
        return (jnp.arange(entries.shape[position]) // (entries.shape[position] // parts)).reshape((-1,) + (1,) * (entries.ndim - 1 - position))

    one_side = jax.random.permutation(stream_key, parts)[block_of(target)]
    other_side = (block_of(target) + parts // 2) % parts
    return jnp.where((block_of(source) == one_side) | (block_of(source) == other_side), factor * entries, entries)


def level_of(stream_key, dims, cuts, low, largest):
    def one(axis_at, shards_of):
        heights = jax.random.uniform(jax.random.fold_in(jax.random.fold_in(stream_key, 6), axis_at), (shards_of,), jnp.float32, low / len(cuts), largest / len(cuts))
        return jnp.repeat(jnp.exp(heights), dims[axis_at] // shards_of).reshape((-1,) + (1,) * (len(dims) - axis_at - 1))

    loudness = one(*cuts[0])
    for cut in cuts[1:]:
        loudness = loudness * one(*cut)
    return loudness


def gaussian(rng, extent, scale, limit, cuts=(), kind=jnp.bfloat16):
    entries = scale * jax.random.normal(rng, extent, jnp.float32)
    if cuts:
        entries = entries * level_of(rng, extent, cuts, -0.22, 0.18)
    return jnp.clip(entries, -limit, limit).astype(kind)


def bell_draw_with(rng, dims, deviation, reach, shards, heavy, kind=jnp.bfloat16):
    array = deviation * jax.random.normal(rng, dims, jnp.float32)
    if shards:
        array = array * level_of(rng, dims, shards, -0.22, 0.18)
    return jnp.clip(raised(array, jax.random.fold_in(rng, 3), *heavy), -reach, reach).astype(kind)


def setup_inputs(seed: int = 0, part: int = 0) -> dict:
    key_list = jax.random.split(jax.random.key(seed), 8)
    part_splits = jax.random.split(jax.random.fold_in(key_list[7], part), 8)
    return {
        "right_side": gaussian(part_splits[0], (SUBDOMAINS, IFACE_ROWS, ALL_MODES), 1.0, 6.0, ((0, 8), (2, 2))),
        "interface_inverse": gaussian(part_splits[1], (SUBDOMAINS, IFACE_ROWS, IFACE_ROWS), IFACE_ROWS ** -0.5, 0.1875, ((0, 8),)),
        "coupling": jnp.clip(0.5 + 1.5 * jax.random.uniform(part_splits[2], (SUBDOMAINS, 2, FACE_ROWS), jnp.float32) ** level_of(part_splits[2], (SUBDOMAINS, 2, FACE_ROWS), ((0, 8),), -0.2, 0.2), 0.5, 2.0),
        "trace_rows": touch_ends(jax.random.randint(part_splits[3], (SUBDOMAINS, 2, FACE_ROWS), 0, IFACE_ROWS), jax.random.fold_in(part_splits[3], 1), 0, IFACE_ROWS - 1).astype(jnp.int32),
        "deflation_basis": gaussian(part_splits[4], (SUBDOMAINS, IFACE_ROWS, DEFL_SLOTS), (IFACE_ROWS // 4) ** -0.5, 0.375, ((0, 8),)),
        "deflation_counts": draw_deflation_counts(jax.random.fold_in(jax.random.fold_in(key_list[7], part), 71), part),
        "coarse_inverse": bell_draw_with(part_splits[6], (N_SUB, N_TILE, DEFL_SLOTS, N_SUB, N_TILE * DEFL_SLOTS), COARSE_ORDER ** -0.5, 0.25, ((1, 2), (2, 2), (3, 4)), (3, 0, 4, 2.0)),
    }


def batched_product(left_stack, right_stack):
    return lax.map(lambda operands: jnp.dot(operands[0], operands[1], preferred_element_type=jnp.float32), (left_stack, right_stack))


def reference(right_side, interface_inverse, coupling, trace_rows, deflation_basis, deflation_counts, coarse_inverse):
    slot_ids = jnp.arange(DEFL_SLOTS, dtype=jnp.int32)
    live_slots = slot_ids[None, :] < deflation_counts[:, None]
    masked_basis = jnp.where(live_slots[:, None, :], deflation_basis, jnp.zeros((), deflation_basis.dtype))
    basis_rows = jnp.swapaxes(masked_basis, 1, 2)
    coarse_columns = coarse_inverse.reshape(COARSE_ORDER, N_SUB, N_TILE * DEFL_SLOTS)
    source = right_side.astype(jnp.float32)
    iterate = jnp.zeros((SUBDOMAINS, IFACE_ROWS, ALL_MODES), jnp.float32)
    zero_face = jnp.zeros((1, FACE_ROWS, ALL_MODES), jnp.float32)
    for cycle_index in range(ROUNDS):
        lower_trace = jnp.take_along_axis(iterate, trace_rows[:, 0, :, None], axis=1)
        upper_trace = jnp.take_along_axis(iterate, trace_rows[:, 1, :, None], axis=1)
        from_lower = jnp.concatenate([zero_face, upper_trace[:-1]], axis=0)
        from_upper = jnp.concatenate([lower_trace[1:], zero_face], axis=0)
        lower_rows = source[:, :FACE_ROWS] + coupling[:, 0, :, None] * from_lower
        upper_rows = source[:, IFACE_ROWS - FACE_ROWS:] + coupling[:, 1, :, None] * from_upper
        boundary = jnp.concatenate([lower_rows, source[:, FACE_ROWS:IFACE_ROWS - FACE_ROWS], upper_rows], axis=1).astype(jnp.bfloat16)
        local_solve = batched_product(interface_inverse, boundary)
        defect = (local_solve - iterate).astype(jnp.bfloat16)
        projected = batched_product(basis_rows, defect).astype(jnp.bfloat16)
        vector = projected.reshape(N_SUB, N_TILE * DEFL_SLOTS, ALL_MODES)

        def add_part(total, index):
            columns = lax.dynamic_index_in_dim(coarse_columns, index, 1, keepdims=False)
            inputs = lax.dynamic_index_in_dim(vector, index, 0, keepdims=False)
            part = jnp.dot(columns, inputs, preferred_element_type=jnp.float32).astype(jnp.bfloat16)
            part = lax.optimization_barrier(part)
            return total + part.astype(jnp.float32), None

        start_total = jnp.zeros((COARSE_ORDER, ALL_MODES), jnp.float32)
        total, unused = lax.scan(add_part, start_total, jnp.arange(N_SUB, dtype=jnp.int32))
        coarse = total.astype(jnp.bfloat16).reshape(SUBDOMAINS, DEFL_SLOTS, ALL_MODES)
        iterate = local_solve + batched_product(masked_basis, coarse)
    return iterate.astype(jnp.bfloat16)
```

```python
import functools

import jax
import jax.numpy as jnp
from jax import lax
from jax.experimental import pallas as pl
from jax.experimental.pallas import tpu as pltpu
from jax.sharding import PartitionSpec as P

MESH = pl.DeviceIdType.MESH
ROW_TILES = 4
BF16 = jnp.bfloat16
F32 = jnp.float32


def mm(a, b):
    return jnp.dot(a, b, preferred_element_type=F32)


def middle_first(n):
    return sorted(range(1, n), key=lambda k: abs(2 * k - n))


def kernel(
    n_sub,
    n_tile,
    n_rep,
    source_hbm,
    inverse_hbm,
    coupling_ref,
    rows_ref,
    basis_hbm,
    counts_ref,
    coarse_hbm,
    out_hbm,
    source,
    inverse,
    basis,
    basis_t,
    coarse,
    solve,
    face_inverse,
    picked,
    blocks,
    shares,
    arrived,
    traces,
    halo,
    out,
    load_sem,
    inverse_sem,
    out_sem,
    rep_send,
    rep_recv,
    tile_send,
    tile_recv,
    sub_send,
    sub_recv,
    halo_send,
    halo_recv,
):
    j = lax.axis_index("sub")
    t = lax.axis_index("tile")
    r = lax.axis_index("rep")
    s = j * n_tile + t
    n_all = n_sub * n_tile
    slots = basis.shape[1]
    face = halo.shape[1]
    iface = source.shape[0]
    half = coarse_hbm.shape[1]
    chunk = iface // ROW_TILES

    has_lower = s > 0
    has_upper = s < n_all - 1
    below = lax.rem(s + n_all - 1, n_all)
    above = lax.rem(s + 1, n_all)
    lower_id = {"sub": lax.div(below, n_tile), "tile": lax.rem(below, n_tile)}
    upper_id = {"sub": lax.div(above, n_tile), "tile": lax.rem(above, n_tile)}

    def at_offset(axis, me, n, k):
        return {axis: lax.rem(me + k, n)}

    half_rows = pl.ds(pl.multiple_of(r * half, half), half)
    load_basis = pltpu.make_async_copy(basis_hbm, basis, load_sem.at[0])
    load_source = pltpu.make_async_copy(source_hbm, source, load_sem.at[1])
    load_coarse = pltpu.make_async_copy(coarse_hbm, coarse.at[:, half_rows, :], load_sem.at[2])
    load_basis.start()
    load_source.start()
    loads = []
    for i in range(ROW_TILES):
        part = pl.ds(i * chunk, chunk)
        loads.append(pltpu.make_async_copy(inverse_hbm.at[part], inverse.at[part], inverse_sem.at[i]))
        loads[-1].start()
    load_coarse.start()

    barrier = pltpu.get_barrier_semaphore()
    peers = [at_offset("rep", r, n_rep, k) for k in range(1, n_rep)]
    peers += [at_offset("tile", t, n_tile, k) for k in range(1, n_tile)]
    peers += [at_offset("sub", j, n_sub, k) for k in range(1, n_sub)]
    peers += [lower_id, upper_id]
    for peer in peers:
        pl.semaphore_signal(barrier, inc=1, device_id=peer, device_id_type=MESH)

    load_basis.wait()
    slot_ids = lax.broadcasted_iota(jnp.int32, (iface, slots), 1)
    live = slot_ids < counts_ref[0]
    basis[...] = jnp.where(live, basis[...].astype(F32), 0.0).astype(BF16)
    basis_t[...] = basis[...].astype(F32).T.astype(BF16)

    pl.semaphore_wait(barrier, len(peers))
    rep_copies = []
    for k in range(1, n_rep):
        copy = pltpu.make_async_remote_copy(
            src_ref=coarse_hbm,
            dst_ref=coarse.at[:, half_rows, :],
            send_sem=rep_send.at[k],
            recv_sem=rep_recv.at[k],
            device_id=at_offset("rep", r, n_rep, k),
            device_id_type=MESH,
        )
        copy.start()
        rep_copies.append(copy)

    load_source.wait()
    projected = jnp.zeros((slots, source.shape[1]), F32)
    for i in range(ROW_TILES):
        part = pl.ds(i * chunk, chunk)
        loads[i].wait()
        piece = mm(inverse[part, :], source[...])
        solve[part, :] = piece
        projected += mm(basis_t[:, part], piece.astype(BF16))

    def start_blocks(which, value):
        mine = pl.ds(pl.multiple_of(t * slots, slots), slots)
        blocks[which, mine, :] = value.astype(BF16)
        copies = []
        for k in range(1, n_tile):
            copy = pltpu.make_async_remote_copy(
                src_ref=blocks.at[which, mine],
                dst_ref=blocks.at[which, mine],
                send_sem=tile_send.at[which, k],
                recv_sem=tile_recv.at[which, k],
                device_id=at_offset("tile", t, n_tile, k),
                device_id_type=MESH,
            )
            copy.start()
            copies.append(copy)
        return copies

    def start_shares(which):
        copies = []
        for k in middle_first(n_sub):
            target = lax.rem(j + k, n_sub)
            shares[which, k] = mm(coarse[target], blocks[which]).astype(BF16)
            copy = pltpu.make_async_remote_copy(
                src_ref=shares.at[which, k],
                dst_ref=arrived.at[which, k],
                send_sem=sub_send.at[which, k],
                recv_sem=sub_recv.at[which, k],
                device_id=at_offset("sub", j, n_sub, k),
                device_id_type=MESH,
            )
            copy.start()
            copies.append(copy)
        return copies, mm(coarse[j], blocks[which])

    def summed(which, copies, total):
        for k, copy in zip(middle_first(n_sub), copies):
            copy.wait_recv()
            total += arrived[which, k].astype(F32)
        return total.astype(BF16)

    sends = list(rep_copies)
    tile_copies = start_blocks(0, projected)
    sends += tile_copies
    load_coarse.wait()
    face_inverse[:, :face] = (inverse[:, :face].astype(F32) * coupling_ref[0:1, :]).astype(BF16)
    face_inverse[:, face:] = (inverse[:, iface - face :].astype(F32) * coupling_ref[1:2, :]).astype(BF16)
    for copy in rep_copies + tile_copies:
        copy.wait_recv()
    sub_copies, total = start_shares(0)
    sends += sub_copies

    row_ids = lax.broadcasted_iota(jnp.int32, (iface, face), 0)
    for f in range(2):
        chosen = jnp.where(row_ids == rows_ref[f : f + 1, :], 1.0, 0.0)
        picked[pl.ds(f * face, face), :] = chosen.T.astype(BF16)
    trace_solve = mm(picked[...], solve[...].astype(BF16))
    trace_basis = mm(picked[...], basis[...]).astype(BF16)
    gram = mm(basis_t[...], basis[...]).astype(BF16)
    face_product = mm(basis_t[...], face_inverse[...]).astype(BF16)

    own = summed(0, sub_copies, total)
    traces[...] = (trace_solve + mm(trace_basis, own)).astype(BF16)

    to_upper = pltpu.make_async_remote_copy(
        src_ref=traces.at[pl.ds(face, face)],
        dst_ref=halo.at[0],
        send_sem=halo_send.at[0],
        recv_sem=halo_recv.at[0],
        device_id=upper_id,
        device_id_type=MESH,
    )
    to_lower = pltpu.make_async_remote_copy(
        src_ref=traces.at[pl.ds(0, face)],
        dst_ref=halo.at[1],
        send_sem=halo_send.at[1],
        recv_sem=halo_recv.at[1],
        device_id=lower_id,
        device_id_type=MESH,
    )

    @pl.when(has_upper)
    def _():
        to_upper.start()

    @pl.when(has_lower)
    def _():
        to_lower.start()

    @pl.when(jnp.logical_not(has_lower))
    def _():
        halo[0] = jnp.zeros(halo.shape[1:], BF16)

    @pl.when(jnp.logical_not(has_upper))
    def _():
        halo[1] = jnp.zeros(halo.shape[1:], BF16)

    step = mm(gram, own)

    @pl.when(has_lower)
    def _():
        to_upper.wait_recv()

    @pl.when(has_upper)
    def _():
        to_lower.wait_recv()

    projected = mm(face_product[:, :face], halo[0]) + mm(face_product[:, face:], halo[1]) - step
    tile_copies = start_blocks(1, projected)
    sends += tile_copies
    for copy in tile_copies:
        copy.wait_recv()
    sub_copies, total = start_shares(1)
    sends += sub_copies
    for i in range(ROW_TILES):
        part = pl.ds(i * chunk, chunk)
        solve[part, :] = (
            solve[part, :]
            + mm(face_inverse[part, :face], halo[0])
            + mm(face_inverse[part, face:], halo[1])
        )
    own = summed(1, sub_copies, total)
    stores = []
    for i in range(ROW_TILES):
        part = pl.ds(i * chunk, chunk)
        out[part, :] = (solve[part, :] + mm(basis[part, :], own)).astype(BF16)
        stores.append(pltpu.make_async_copy(out.at[part], out_hbm.at[part], out_sem.at[i]))
        stores[-1].start()

    @pl.when(has_upper)
    def _():
        to_upper.wait_send()

    @pl.when(has_lower)
    def _():
        to_lower.wait_send()

    for copy in sends:
        copy.wait_send()
    for store in stores:
        store.wait()


def local(
    n_sub,
    n_tile,
    n_rep,
    right_side,
    interface_inverse,
    coupling,
    trace_rows,
    deflation_basis,
    deflation_counts,
    coarse_inverse,
):
    source = right_side[0]
    iface, modes = source.shape
    face = coupling.shape[2]
    slots = deflation_basis.shape[2]
    half = coarse_inverse.shape[2]
    inputs = coarse_inverse.shape[4]
    coarse_block = coarse_inverse.reshape(n_sub, half, inputs)
    hbm = pl.BlockSpec(memory_space=pl.ANY)
    vmem = pl.BlockSpec(memory_space=pltpu.VMEM)
    smem = pl.BlockSpec(memory_space=pltpu.SMEM)
    dma = pltpu.SemaphoreType.DMA
    macs = modes * (iface * iface + 6 * iface * slots + 2 * n_sub * slots * inputs)
    field = pl.pallas_call(
        functools.partial(kernel, n_sub, n_tile, n_rep),
        out_shape=jax.ShapeDtypeStruct((iface, modes), BF16),
        in_specs=[hbm, hbm, vmem, vmem, hbm, smem, hbm],
        out_specs=hbm,
        scratch_shapes=[
            pltpu.VMEM((iface, modes), BF16),
            pltpu.VMEM((iface, iface), BF16),
            pltpu.VMEM((iface, slots), BF16),
            pltpu.VMEM((slots, iface), BF16),
            pltpu.VMEM((n_sub, slots, inputs), BF16),
            pltpu.VMEM((iface, modes), F32),
            pltpu.VMEM((iface, 2 * face), BF16),
            pltpu.VMEM((2 * face, iface), BF16),
            pltpu.VMEM((2, inputs, modes), BF16),
            pltpu.VMEM((2, n_sub, slots, modes), BF16),
            pltpu.VMEM((2, n_sub, slots, modes), BF16),
            pltpu.VMEM((2 * face, modes), BF16),
            pltpu.VMEM((2, face, modes), BF16),
            pltpu.VMEM((iface, modes), BF16),
            dma((3,)),
            dma((ROW_TILES,)),
            dma((ROW_TILES,)),
            dma((n_rep,)),
            dma((n_rep,)),
            dma((2, n_tile)),
            dma((2, n_tile)),
            dma((2, n_sub)),
            dma((2, n_sub)),
            dma((2,)),
            dma((2,)),
        ],
        compiler_params=pltpu.CompilerParams(
            collective_id=0, has_side_effects=True, vmem_limit_bytes=56 * 1024 * 1024
        ),
        cost_estimate=pl.CostEstimate(
            flops=2 * macs, bytes_accessed=2 * iface * (iface + 2 * modes + slots), transcendentals=0
        ),
    )(
        source,
        interface_inverse[0],
        coupling[0],
        trace_rows[0],
        deflation_basis[0],
        deflation_counts,
        coarse_block,
    )
    return field[None]


def solution(mesh):
    placed = (
        P(("group", "sub", "tile"), None, "rep"),
        P(("group", "sub", "tile"), None, None),
        P(("group", "sub", "tile"), None, None),
        P(("group", "sub", "tile"), None, None),
        P(("group", "sub", "tile"), None, None),
        P(("group", "sub", "tile")),
        P("group", "tile", "rep", "sub", None),
    )
    return jax.shard_map(
        functools.partial(local, mesh.shape["sub"], mesh.shape["tile"], mesh.shape["rep"]),
        mesh=mesh,
        in_specs=placed,
        out_specs=P(("group", "sub", "tile"), None, "rep"),
        check_vma=False,
    )
```

```python
import functools

import jax
import jax.numpy as jnp
from jax import lax
from jax.experimental import pallas as pl
from jax.experimental.pallas import tpu as pltpu
from jax.sharding import PartitionSpec as P

MESH = pl.DeviceIdType.MESH
ROW_TILES = 4
BF16 = jnp.bfloat16
F32 = jnp.float32


def mm(a, b):
    return jnp.dot(a, b, preferred_element_type=F32)


def middle_first(n):
    return sorted(range(1, n), key=lambda k: abs(2 * k - n))


def kernel(
    n_sub,
    n_tile,
    n_rep,
    pack,
    source_hbm,
    inverse_hbm,
    coupling_ref,
    rows_ref,
    basis_hbm,
    counts_ref,
    coarse_hbm,
    out_hbm,
    source,
    inverse,
    basis,
    basis_t,
    coarse,
    solve,
    face_inverse,
    picked,
    blocks,
    shares,
    arrived,
    traces,
    halo,
    out,
    load_sem,
    inverse_sem,
    out_sem,
    rep_send,
    rep_recv,
    relay_send,
    relay_recv,
    pack_send,
    pack_recv,
    block_send,
    block_recv,
    sub_send,
    sub_recv,
    halo_send,
    halo_recv,
):
    j = lax.axis_index("sub")
    t = lax.axis_index("tile")
    r = lax.axis_index("rep")
    s = j * n_tile + t
    n_all = n_sub * n_tile
    slots = basis.shape[1]
    face = halo.shape[1]
    iface = source.shape[0]
    half = coarse_hbm.shape[2]
    inputs = coarse_hbm.shape[3]
    n_packs = n_sub // pack
    mine = lax.div(j, pack)
    i = lax.rem(j, pack)
    chunk = iface // ROW_TILES

    has_lower = s > 0
    has_upper = s < n_all - 1
    below = lax.rem(s + n_all - 1, n_all)
    above = lax.rem(s + 1, n_all)
    lower_id = {"sub": lax.div(below, n_tile), "tile": lax.rem(below, n_tile)}
    upper_id = {"sub": lax.div(above, n_tile), "tile": lax.rem(above, n_tile)}

    def rep_id(k):
        return {"rep": lax.rem(r + k, n_rep)}

    def pack_id(k, k_tile):
        return {"sub": mine * pack + lax.rem(i + k, pack), "tile": lax.rem(t + k_tile, n_tile)}

    def share_id(k):
        return {"sub": lax.rem(mine + k, n_packs) * pack + i}

    def pack_columns(k):
        return pl.ds(pl.multiple_of(lax.rem(i + k, pack) * inputs, inputs), inputs)

    square = [(a, b) for a in range(pack) for b in range(n_tile) if a or b][::-1]

    half_rows = pl.ds(pl.multiple_of(r * half, half), half)
    load_basis = pltpu.make_async_copy(basis_hbm, basis, load_sem.at[0])
    load_source = pltpu.make_async_copy(source_hbm, source, load_sem.at[1])
    load_coarse = pltpu.make_async_copy(
        coarse_hbm.at[:, i], coarse.at[:, half_rows, pack_columns(0)], load_sem.at[2]
    )
    load_basis.start()
    load_source.start()
    loads = []
    for q in range(ROW_TILES):
        part = pl.ds(q * chunk, chunk)
        loads.append(pltpu.make_async_copy(inverse_hbm.at[part], inverse.at[part], inverse_sem.at[q]))
        loads[-1].start()
    load_coarse.start()

    barrier = pltpu.get_barrier_semaphore()
    peers = [rep_id(k) for k in range(1, n_rep)]
    peers += [pack_id(a, b) for a, b in square]
    peers += [share_id(k) for k in range(1, n_packs)]
    peers += [lower_id, upper_id]
    for peer in peers:
        pl.semaphore_signal(barrier, inc=1, device_id=peer, device_id_type=MESH)

    load_basis.wait()
    slot_ids = lax.broadcasted_iota(jnp.int32, (iface, slots), 1)
    live = slot_ids < counts_ref[0]
    basis[...] = jnp.where(live, basis[...].astype(F32), 0.0).astype(BF16)
    basis_t[...] = basis[...].astype(F32).T.astype(BF16)

    pl.semaphore_wait(barrier, len(peers))
    pack_copies = []
    for k in range(1, pack):
        copy = pltpu.make_async_remote_copy(
            src_ref=coarse_hbm.at[:, lax.rem(i + k, pack)],
            dst_ref=coarse.at[:, half_rows, pack_columns(0)],
            send_sem=pack_send.at[k],
            recv_sem=pack_recv.at[k],
            device_id=pack_id(k, 0),
            device_id_type=MESH,
        )
        copy.start()
        pack_copies.append(copy)
    rep_copies = []
    for k in range(1, n_rep):
        copy = pltpu.make_async_remote_copy(
            src_ref=coarse_hbm.at[:, i],
            dst_ref=coarse.at[:, half_rows, pack_columns(0)],
            send_sem=rep_send.at[k],
            recv_sem=rep_recv.at[k],
            device_id=rep_id(k),
            device_id_type=MESH,
        )
        copy.start()
        rep_copies.append(copy)

    load_source.wait()
    projected = jnp.zeros((slots, source.shape[1]), F32)
    for q in range(ROW_TILES):
        part = pl.ds(q * chunk, chunk)
        loads[q].wait()
        piece = mm(inverse[part, :], source[...])
        solve[part, :] = piece
        projected += mm(basis_t[:, part], piece.astype(BF16))

    def start_blocks(which, value):
        place = pl.ds(pl.multiple_of((i * n_tile + t) * slots, slots), slots)
        blocks[which, place, :] = value.astype(BF16)
        copies = []
        for a, b in square:
            copy = pltpu.make_async_remote_copy(
                src_ref=blocks.at[which, place],
                dst_ref=blocks.at[which, place],
                send_sem=block_send.at[which, a, b],
                recv_sem=block_recv.at[which, a, b],
                device_id=pack_id(a, b),
                device_id_type=MESH,
            )
            copy.start()
            copies.append(copy)
        return copies

    def start_shares(which):
        copies = []
        for k in middle_first(n_packs):
            target = lax.rem(mine + k, n_packs)
            shares[which, k] = mm(coarse[target], blocks[which]).astype(BF16)
            copy = pltpu.make_async_remote_copy(
                src_ref=shares.at[which, k],
                dst_ref=arrived.at[which, k],
                send_sem=sub_send.at[which, k],
                recv_sem=sub_recv.at[which, k],
                device_id=share_id(k),
                device_id_type=MESH,
            )
            copy.start()
            copies.append(copy)
        return copies, mm(coarse[mine], blocks[which])

    def summed(which, copies, total):
        for k, copy in zip(middle_first(n_packs), copies):
            copy.wait_recv()
            total += arrived[which, k].astype(F32)
        return total.astype(BF16)

    sends = rep_copies + pack_copies
    block_copies = start_blocks(0, projected)
    sends += block_copies
    relays = []
    for k, arriving in zip(range(1, pack), pack_copies):
        arriving.wait_recv()
        piece = coarse.at[:, half_rows, pack_columns(pack - k)]
        for m in range(1, n_rep):
            copy = pltpu.make_async_remote_copy(
                src_ref=piece,
                dst_ref=piece,
                send_sem=relay_send.at[k, m],
                recv_sem=relay_recv.at[k, m],
                device_id=rep_id(m),
                device_id_type=MESH,
            )
            copy.start()
            relays.append(copy)
    sends += relays
    load_coarse.wait()
    face_inverse[:, :face] = (inverse[:, :face].astype(F32) * coupling_ref[0:1, :]).astype(BF16)
    face_inverse[:, face:] = (inverse[:, iface - face :].astype(F32) * coupling_ref[1:2, :]).astype(BF16)
    for copy in rep_copies + relays + block_copies:
        copy.wait_recv()
    sub_copies, total = start_shares(0)
    sends += sub_copies

    row_ids = lax.broadcasted_iota(jnp.int32, (iface, face), 0)
    for f in range(2):
        chosen = jnp.where(row_ids == rows_ref[f : f + 1, :], 1.0, 0.0)
        picked[pl.ds(f * face, face), :] = chosen.T.astype(BF16)
    trace_solve = mm(picked[...], solve[...].astype(BF16))
    trace_basis = mm(picked[...], basis[...]).astype(BF16)
    gram = mm(basis_t[...], basis[...]).astype(BF16)
    face_product = mm(basis_t[...], face_inverse[...]).astype(BF16)

    own = summed(0, sub_copies, total)
    traces[...] = (trace_solve + mm(trace_basis, own)).astype(BF16)

    to_upper = pltpu.make_async_remote_copy(
        src_ref=traces.at[pl.ds(face, face)],
        dst_ref=halo.at[0],
        send_sem=halo_send.at[0],
        recv_sem=halo_recv.at[0],
        device_id=upper_id,
        device_id_type=MESH,
    )
    to_lower = pltpu.make_async_remote_copy(
        src_ref=traces.at[pl.ds(0, face)],
        dst_ref=halo.at[1],
        send_sem=halo_send.at[1],
        recv_sem=halo_recv.at[1],
        device_id=lower_id,
        device_id_type=MESH,
    )

    @pl.when(has_upper)
    def _():
        to_upper.start()

    @pl.when(has_lower)
    def _():
        to_lower.start()

    @pl.when(jnp.logical_not(has_lower))
    def _():
        halo[0] = jnp.zeros(halo.shape[1:], BF16)

    @pl.when(jnp.logical_not(has_upper))
    def _():
        halo[1] = jnp.zeros(halo.shape[1:], BF16)

    step = mm(gram, own)

    @pl.when(has_lower)
    def _():
        to_upper.wait_recv()

    @pl.when(has_upper)
    def _():
        to_lower.wait_recv()

    projected = mm(face_product[:, :face], halo[0]) + mm(face_product[:, face:], halo[1]) - step
    block_copies = start_blocks(1, projected)
    sends += block_copies
    for copy in block_copies:
        copy.wait_recv()
    sub_copies, total = start_shares(1)
    sends += sub_copies
    for q in range(ROW_TILES):
        part = pl.ds(q * chunk, chunk)
        solve[part, :] = (
            solve[part, :]
            + mm(face_inverse[part, :face], halo[0])
            + mm(face_inverse[part, face:], halo[1])
        )
    own = summed(1, sub_copies, total)
    stores = []
    for q in range(ROW_TILES):
        part = pl.ds(q * chunk, chunk)
        out[part, :] = (solve[part, :] + mm(basis[part, :], own)).astype(BF16)
        stores.append(pltpu.make_async_copy(out.at[part], out_hbm.at[part], out_sem.at[q]))
        stores[-1].start()

    @pl.when(has_upper)
    def _():
        to_upper.wait_send()

    @pl.when(has_lower)
    def _():
        to_lower.wait_send()

    for copy in sends:
        copy.wait_send()
    for store in stores:
        store.wait()


def local(
    n_sub,
    n_tile,
    n_rep,
    right_side,
    interface_inverse,
    coupling,
    trace_rows,
    deflation_basis,
    deflation_counts,
    coarse_inverse,
):
    source = right_side[0]
    iface, modes = source.shape
    face = coupling.shape[2]
    slots = deflation_basis.shape[2]
    half = coarse_inverse.shape[2]
    inputs = coarse_inverse.shape[4]
    pack = 2 if n_sub % 2 == 0 else 1
    n_packs = n_sub // pack
    coarse_block = coarse_inverse.reshape(n_packs, pack, half, inputs)
    hbm = pl.BlockSpec(memory_space=pl.ANY)
    vmem = pl.BlockSpec(memory_space=pltpu.VMEM)
    smem = pl.BlockSpec(memory_space=pltpu.SMEM)
    dma = pltpu.SemaphoreType.DMA
    macs = modes * (iface * iface + 6 * iface * slots + 2 * n_sub * slots * inputs)
    field = pl.pallas_call(
        functools.partial(kernel, n_sub, n_tile, n_rep, pack),
        out_shape=jax.ShapeDtypeStruct((iface, modes), BF16),
        in_specs=[hbm, hbm, vmem, vmem, hbm, smem, hbm],
        out_specs=hbm,
        scratch_shapes=[
            pltpu.VMEM((iface, modes), BF16),
            pltpu.VMEM((iface, iface), BF16),
            pltpu.VMEM((iface, slots), BF16),
            pltpu.VMEM((slots, iface), BF16),
            pltpu.VMEM((n_packs, slots, pack * inputs), BF16),
            pltpu.VMEM((iface, modes), F32),
            pltpu.VMEM((iface, 2 * face), BF16),
            pltpu.VMEM((2 * face, iface), BF16),
            pltpu.VMEM((2, pack * inputs, modes), BF16),
            pltpu.VMEM((2, n_packs, slots, modes), BF16),
            pltpu.VMEM((2, n_packs, slots, modes), BF16),
            pltpu.VMEM((2 * face, modes), BF16),
            pltpu.VMEM((2, face, modes), BF16),
            pltpu.VMEM((iface, modes), BF16),
            dma((3,)),
            dma((ROW_TILES,)),
            dma((ROW_TILES,)),
            dma((n_rep,)),
            dma((n_rep,)),
            dma((pack, n_rep)),
            dma((pack, n_rep)),
            dma((pack,)),
            dma((pack,)),
            dma((2, pack, n_tile)),
            dma((2, pack, n_tile)),
            dma((2, n_packs)),
            dma((2, n_packs)),
            dma((2,)),
            dma((2,)),
        ],
        compiler_params=pltpu.CompilerParams(
            collective_id=0, has_side_effects=True, vmem_limit_bytes=56 * 1024 * 1024
        ),
        cost_estimate=pl.CostEstimate(
            flops=2 * macs, bytes_accessed=2 * iface * (iface + 2 * modes + slots), transcendentals=0
        ),
    )(
        source,
        interface_inverse[0],
        coupling[0],
        trace_rows[0],
        deflation_basis[0],
        deflation_counts,
        coarse_block,
    )
    return field[None]


def solution(mesh):
    placed = (
        P(("group", "sub", "tile"), None, "rep"),
        P(("group", "sub", "tile"), None, None),
        P(("group", "sub", "tile"), None, None),
        P(("group", "sub", "tile"), None, None),
        P(("group", "sub", "tile"), None, None),
        P(("group", "sub", "tile")),
        P("group", "tile", "rep", "sub", None),
    )
    return jax.shard_map(
        functools.partial(local, mesh.shape["sub"], mesh.shape["tile"], mesh.shape["rep"]),
        mesh=mesh,
        in_specs=placed,
        out_specs=P(("group", "sub", "tile"), None, "rep"),
        check_vma=False,
    )
```
